256 devices in a mesh: row: 32 (over x, y, core), col: 8 (over z).
Axes of the slice: x: 4, y: 4, z: 8, core: 2. Of those that a mesh axis runs over, the one named last changes fastest.
Arguments:
- tokens: bfloat16 [1024, 12288], P('row', 'col'), may hold values from -6 to 6
- weight: bfloat16 [12288, 49152], P('col', 'row'), may hold values from -0.0546875 to 0.0546875
- grad_out: bfloat16 [1024, 49152], P('col', 'row'), may hold values from -6 to 6
Outputs:
- hidden: bfloat16 [1024, 49152], P('col', 'row')
- grad_tokens: bfloat16 [1024, 12288], P('row', 'col')
- grad_weight: bfloat16 [12288, 49152], P('col', 'row')
The draws below stay inside these ranges and needn't reach their ends.
All inputs are finite; a program needn't handle non-finite values.
Results may differ from the reference program's by a relative error of at most 0.024.
Values may be sent and summed in bfloat16 or wider, within the bound.
A program may use at most 64 MiB of HBM per device.

```python
import math
import jax
import jax.numpy as jnp
from jax import lax

D = 12288
FF = 49152
TOKENS = 1024
N_ROW = 32
N_COL = 8


def shard_levels(own_key, dims, shards, smallest, largest):
    factor_of, own = 1.0, jax.random.fold_in(own_key, 6)
    for axis_at, blocks in shards:
        draws = jnp.exp(jax.random.uniform(jax.random.fold_in(own, axis_at), (blocks,), jnp.float32, smallest / len(shards), largest / len(shards)))
        factor_of = factor_of * jnp.repeat(draws, dims[axis_at] // blocks).reshape([-1 if axis == axis_at else 1 for axis in range(len(dims))])
    return factor_of


def bell_draw(own_key, shape, deviation, limit, cuts=(), held_as=jnp.bfloat16):
    array = jax.random.normal(own_key, shape, jnp.float32) * deviation
    if len(cuts) > 0:
        array = shard_levels(own_key, shape, cuts, -0.22, 0.18) * array
    return jnp.clip(array, min=-limit, max=limit).astype(held_as)


def setup_inputs(seed: int = 0) -> dict:
    arg_keys = jax.random.split(jax.random.key(seed), 4)
    tokens = bell_draw(arg_keys[0], (TOKENS, D), 1.0, 6.0, ((0, 32), (1, 8)))
    weight = bell_draw(arg_keys[1], (D, FF), D ** -0.5, 0.0546875, ((0, 8), (1, 32)))
    grad_out = bell_draw(arg_keys[2], (TOKENS, FF), 1.0, 6.0, ((0, 8), (1, 32)))
    return {"tokens": tokens, "weight": weight, "grad_out": grad_out}


def activations(pre):
    coef = math.sqrt(2.0 / math.pi)
    inner = coef * (pre + 0.044715 * pre * pre * pre)
    tval = jnp.tanh(inner)
    hidden = 0.5 * pre * (1.0 + tval)
    slope = 0.5 * (1.0 + tval) + 0.5 * pre * (1.0 - tval * tval) * coef * (1.0 + 3.0 * 0.044715 * pre * pre)
    return (hidden, slope)

def rounded(value):
    return lax.optimization_barrier(value.astype(jnp.bfloat16)).astype(jnp.float32)

def reference(tokens, weight, grad_out):
    feat_block = D // N_COL
    pre = jnp.zeros((tokens.shape[0], weight.shape[1]), jnp.float32)
    for block in range(N_COL):
        left = tokens[:, block * feat_block:(block + 1) * feat_block]
        right = weight[block * feat_block:(block + 1) * feat_block, :]
        pre = pre + rounded(jnp.dot(left, right, preferred_element_type=jnp.float32))
    hidden, slope = activations(pre)
    grad_pre = (grad_out.astype(jnp.float32) * slope).astype(jnp.bfloat16)
    unit_block = FF // N_ROW
    grad_tokens = jnp.zeros(tokens.shape, jnp.float32)
    for block in range(N_ROW):
        left = grad_pre[:, block * unit_block:(block + 1) * unit_block]
        right = weight[:, block * unit_block:(block + 1) * unit_block]
        grad_tokens = grad_tokens + rounded(jnp.dot(left, right.T, preferred_element_type=jnp.float32))
    grad_weight = jnp.dot(tokens.T, grad_pre, preferred_element_type=jnp.float32).astype(jnp.bfloat16)
    return (hidden.astype(jnp.bfloat16), grad_tokens.astype(jnp.bfloat16), grad_weight)
```

```python
import math

import jax
import jax.numpy as jnp
from jax import lax
from jax.experimental import pallas as pl
from jax.experimental.pallas import tpu as pltpu
from jax.sharding import PartitionSpec as P

MESH = pl.DeviceIdType.MESH
F32 = jnp.float32
BF16 = jnp.bfloat16
NZ = 8
NC = 8
TB = 16
AHEAD = 1


def activations(pre):
    coef = math.sqrt(2.0 / math.pi)
    inner = coef * (pre + 0.044715 * pre * pre * pre)
    tval = jnp.tanh(inner)
    hidden = 0.5 * pre * (1.0 + tval)
    slope = 0.5 * (1.0 + tval) + 0.5 * pre * (1.0 - tval * tval) * coef * (
        1.0 + 3.0 * 0.044715 * pre * pre
    )
    return (hidden, slope)


def kernel(
    tok_in, w_in, go_in,
    hid_out, gt_out, gw_out,
    w, go, tok, part, ring, gath, quo, quo_in, rs_in, acc,
    tok_send, tok_recv, fwd_send, ring_send, ring_recv, gath_send, gath_recv,
    quo_send, quo_recv, rs_send, rs_recv, load_sem,
):
    row = lax.axis_index("row")
    z = lax.axis_index("col")
    core = lax.rem(row, 2)
    chip = row // 2
    x, y = chip // 4, lax.rem(chip, 4)
    d_me, r_me = row // 4, lax.rem(row, 4)
    sibling = (row + 1 - 2 * core, z)
    hops = ((row, lax.rem(z + 1, NZ)), (row, lax.rem(z + NZ - 1, NZ)))
    dm = tok.shape[-1]
    ff = gath.shape[-1]
    half = ff // 2

    load_w = pltpu.make_async_copy(w_in, w, load_sem.at[0])
    load_go = pltpu.make_async_copy(go_in, go, load_sem.at[1])
    load_w.start()
    load_go.start()

    def plane(j):
        px = lax.rem(x + j // 4, 4)
        py = lax.rem(y + lax.rem(j, 4), 4)
        return ((px * 4 + py) * 2 + core, z)

    barrier = pltpu.get_barrier_semaphore()
    for there in (*hops, sibling):
        pl.semaphore_signal(barrier, inc=1, device_id=there, device_id_type=MESH)

    def greet(j, _):
        pl.semaphore_signal(barrier, inc=1, device_id=plane(j), device_id_type=MESH)
        return 0

    lax.fori_loop(1, 16, greet, 0)
    pl.semaphore_wait(barrier, 18)

    def remote(src, dst, send, recv, there):
        return pltpu.make_async_remote_copy(
            src_ref=src, dst_ref=dst, send_sem=send, recv_sem=recv,
            device_id=there, device_id_type=MESH,
        )

    def send_tokens(c):
        h = c // 4

        @pl.when(r_me == lax.rem(c, 4))
        def _():
            mine = tok_in.at[pl.ds(pl.multiple_of(h * TB, TB), TB)]

            def one(j, _):
                remote(mine, tok.at[c, d_me], tok_send.at[h], tok_recv.at[c], plane(j)).start()
                return 0

            lax.fori_loop(1, 16, one, 0)
            pltpu.make_async_copy(mine, tok.at[c, d_me], tok_recv.at[c]).start()

    def forward_tokens(c):
        return remote(tok.at[c], tok.at[c], fwd_send.at[c], tok_recv.at[c], sibling)

    def ring_copy(d, c, s):
        if s == 0:
            cols = pl.ds(d * half, half)
            src = part.at[c, lax.rem(z + 4, NZ), :, cols]
            dst = ring.at[d, c, 0, :, cols]
        else:
            src, dst = ring.at[d, c, s - 1], ring.at[d, c, s]
        return remote(src, dst, ring_send.at[d, c, s], ring_recv.at[d, c, s], hops[d])

    def gath_copy(d, c, s):
        slot = lax.rem(z + (NZ - s if d == 0 else s), NZ)
        if s == 3:
            ref = gath.at[c, slot, :, pl.ds(d * half, half)]
        else:
            ref = gath.at[c, slot]
        return remote(ref, ref, gath_send.at[d, c, s], gath_recv.at[d, c, s], hops[d])

    def first(c):
        pltpu.make_async_copy(tok.at[c], tok.at[c], tok_recv.at[c]).wait()

        @pl.when(core == lax.rem(c, 2))
        def _():
            forward_tokens(c).start()

        @pl.when(c + AHEAD < NC)
        def _():
            send_tokens(c + AHEAD)

        @pl.when(c == 0)
        def _():
            load_w.wait()

        left = tok[c].reshape(NZ * TB, dm)

        def cols(n, _):
            at = pl.ds(pl.multiple_of(n * 256, 256), 256)
            got = jnp.dot(left, w[:, at], preferred_element_type=F32)
            part[c, :, :, at] = got.astype(BF16).reshape(NZ, TB, 256)
            return 0

        lax.fori_loop(0, ff // 256, cols, 0)
        for d in range(2):
            ring_copy(d, c, 0).start()

    def ring_step(c, s):
        for d in range(2):
            ring_copy(d, c, s - 1).wait_recv()
            at = lax.rem(z + (4 - s if d == 0 else 4 + s), NZ)
            if s == 1:
                got, rest = slice(d * half, (d + 1) * half), slice((1 - d) * half, (2 - d) * half)
                total = ring[d, c, 0, :, got].astype(F32) + part[c, at, :, got].astype(F32)
                ring[d, c, 0, :, got] = total.astype(BF16)
                ring[d, c, 0, :, rest] = part[c, at, :, rest]
            else:
                total = ring[d, c, s - 1].astype(F32) + part[c, at].astype(F32)
                ring[d, c, s - 1] = total.astype(BF16)
            ring_copy(d, c, s).start()

    def middle(c):
        @pl.when(c == 0)
        def _():
            load_go.wait()

        for d in range(2):
            ring_copy(d, c, 3).wait_recv()
        at = pl.ds(pl.multiple_of(lax.rem(c, 4) * 32 + (c // 4) * TB, TB), TB)
        pre = (
            part[c, z].astype(F32) + ring[0, c, 3].astype(F32) + ring[1, c, 3].astype(F32)
        )
        hidden, slope = activations(pre)
        hid_out[at, :] = hidden.astype(BF16)
        gath[c, z] = (go[at, :].astype(F32) * slope).astype(BF16)
        for d in range(2):
            gath_copy(d, c, 0).start()

    def gath_step(c, s):
        for d in range(2):
            gath_copy(d, c, s - 1).wait_recv()
            gath_copy(d, c, s).start()

    def quo_copy(c):
        return remote(quo.at[c], quo_in.at[c], quo_send.at[c], quo_recv.at[c], sibling)

    def back(c):
        for d in range(2):
            gath_copy(d, c, 3).wait_recv()
        left = gath[c].reshape(NZ * TB, ff)

        def cols(n, _):
            at = pl.ds(pl.multiple_of(n * 256, 256), 256)
            got = lax.dot_general(
                left, w[at, :], (((1,), (1,)), ((), ())), preferred_element_type=F32
            )
            quo[c, :, :, at] = got.astype(BF16).reshape(NZ, TB, 256)
            return 0

        lax.fori_loop(0, dm // 256, cols, 0)

        @pl.when(core != lax.rem(c, 2))
        def _():
            quo_copy(c).start()

    def scatter(c):
        r, h = lax.rem(c, 4), c // 4

        @pl.when(core == lax.rem(c, 2))
        def _():
            quo_copy(c).wait_recv()

            def one(j, _):
                at = lax.rem(d_me + j, NZ)
                total = quo[c, at].astype(F32) + quo_in[c, at].astype(F32)
                quo[c, at] = total.astype(BF16)
                there = at * 4 + r

                @pl.when(there != row)
                def _():
                    remote(
                        quo.at[c, at], rs_in.at[h, chip], rs_send.at[c], rs_recv.at[h], (there, z)
                    ).start()

                @pl.when(there == row)
                def _():
                    pltpu.make_async_copy(quo.at[c, at], rs_in.at[h, chip], rs_recv.at[h]).start()

                return 0

            lax.fori_loop(0, NZ, one, 0)

    def weigh(c, n, opening, closing):
        left = tok[pl.ds(c, n)].reshape(n * NZ * TB, dm)
        right = gath[pl.ds(c, n)].reshape(n * NZ * TB, ff)
        for m in range(dm // 256):
            at = pl.ds(m * 256, 256)
            got = lax.dot_general(
                left[:, m * 256 : (m + 1) * 256], right, (((0,), (0,)), ((), ())),
                preferred_element_type=F32,
            )
            if not opening:
                got = got + acc[at, :]
            if closing:
                gw_out[at, :] = got.astype(BF16)
            else:
                acc[at, :] = got

    def collect(h):
        pltpu.make_async_copy(rs_in.at[h], rs_in.at[h], rs_recv.at[h]).wait()
        total = rs_in[h, 0].astype(F32)
        for j in range(1, 16):
            total = total + rs_in[h, j].astype(F32)
        gt_out[pl.ds(h * TB, TB), :] = total.astype(BF16)

    for c in range(AHEAD):
        send_tokens(c)

    def stage(i, offset, fn):
        c = i - offset

        @pl.when((c >= 0) & (c < NC))
        def _():
            fn(jnp.clip(c, 0, NC - 1))

    def step(i, _):
        stage(i, 0, first)
        for s in (1, 2, 3):
            stage(i, s, lambda c: ring_step(c, s))
        stage(i, 4, middle)
        for s in (1, 2, 3):
            stage(i, 4 + s, lambda c: gath_step(c, s))
        stage(i, 8, back)
        stage(i, 9, scatter)

        @pl.when(i == 9)
        def _():
            weigh(0, 2, True, False)

        @pl.when(i == 11)
        def _():
            weigh(2, 2, False, False)

        return 0

    lax.fori_loop(0, NC + 8, step, 0)
    weigh(4, 4, False, True)
    scatter(NC - 1)
    collect(0)
    collect(1)

    for h in range(2):
        sent = rs_in.at[h, pl.ds(0, 15)]
        pltpu.make_async_copy(sent, sent, tok_send.at[h]).wait()

    def drain(c, _):
        for d in range(2):
            for s in range(4):
                ring_copy(d, c, s).wait_send()
                gath_copy(d, c, s).wait_send()
        mine = core == lax.rem(c, 2)

        @pl.when(mine)
        def _():
            forward_tokens(c).wait_send()

        @pl.when(mine & (r_me == lax.rem(c, 4)))
        def _():
            sent = quo_in.at[c, pl.ds(0, 7)]
            pltpu.make_async_copy(sent, sent, rs_send.at[c]).wait()

        @pl.when(mine & (r_me != lax.rem(c, 4)))
        def _():
            sent = quo_in.at[c]
            pltpu.make_async_copy(sent, sent, rs_send.at[c]).wait()

        @pl.when(jnp.logical_not(mine))
        def _():
            quo_copy(c).wait_send()

        return 0

    lax.fori_loop(0, NC, drain, 0)


def local(tokens, weight, grad_out):
    dm, ff = weight.shape
    dma = pltpu.SemaphoreType.DMA
    vmem = pltpu.VMEM
    return pl.pallas_call(
        kernel,
        out_shape=(
            jax.ShapeDtypeStruct(grad_out.shape, BF16),
            jax.ShapeDtypeStruct(tokens.shape, BF16),
            jax.ShapeDtypeStruct(weight.shape, BF16),
        ),
        in_specs=[pl.BlockSpec(memory_space=pl.ANY)] * 3,
        out_specs=[pl.BlockSpec(memory_space=pltpu.VMEM)] * 3,
        scratch_shapes=[
            vmem((dm, ff), BF16),
            vmem(grad_out.shape, BF16),
            vmem((NC, NZ, TB, dm), BF16),
            vmem((NC, NZ, TB, ff), BF16),
            vmem((2, NC, 4, TB, ff), BF16),
            vmem((NC, NZ, TB, ff), BF16),
            vmem((NC, NZ, TB, dm), BF16),
            vmem((NC, NZ, TB, dm), BF16),
            vmem((2, 16, TB, dm), BF16),
            vmem((dm, ff), F32),
            dma((2,)), dma((NC,)), dma((NC,)),
            dma((2, NC, 4)), dma((2, NC, 4)), dma((2, NC, 4)), dma((2, NC, 4)),
            dma((NC,)), dma((NC,)), dma((NC,)), dma((2,)), dma((2,)),
        ],
        compiler_params=pltpu.CompilerParams(
            collective_id=0, has_side_effects=True, vmem_limit_bytes=60 * 1024 * 1024
        ),
        cost_estimate=pl.CostEstimate(
            flops=6 * 1024 * dm * ff, bytes_accessed=4 * dm * ff, transcendentals=0
        ),
        name="mlp",
    )(tokens, weight, grad_out)


def solution(mesh):
    placed = (P("row", "col"), P("col", "row"), P("col", "row"))
    return jax.shard_map(
        local,
        mesh=mesh,
        in_specs=placed,
        out_specs=(P("col", "row"), P("row", "col"), P("col", "row")),
        check_vma=False,
    )
```

```python
import math

import jax
import jax.numpy as jnp
from jax import lax
from jax.experimental import pallas as pl
from jax.experimental.pallas import tpu as pltpu
from jax.sharding import PartitionSpec as P

MESH = pl.DeviceIdType.MESH
F32 = jnp.float32
BF16 = jnp.bfloat16
NZ = 8
NC = 8
TB = 16
AHEAD = 2


def activations(pre):
    coef = math.sqrt(2.0 / math.pi)
    inner = coef * (pre + 0.044715 * pre * pre * pre)
    tval = jnp.tanh(inner)
    hidden = 0.5 * pre * (1.0 + tval)
    slope = 0.5 * (1.0 + tval) + 0.5 * pre * (1.0 - tval * tval) * coef * (
        1.0 + 3.0 * 0.044715 * pre * pre
    )
    return (hidden, slope)


def kernel(
    tok_in, w_in, go_in,
    hid_out, gt_out, gw_out,
    w, wt, go, tok, part, ring, gath, quo, quo_in, rs_in, acc,
    tok_send, tok_recv, fwd_send, fwd_recv, ring_send, ring_recv, gath_send, gath_recv,
    quo_send, quo_recv, rs_send, rs_recv, load_sem,
):
    row = lax.axis_index("row")
    z = lax.axis_index("col")
    core = lax.rem(row, 2)
    chip = row // 2
    x, y = chip // 4, lax.rem(chip, 4)
    d_me, r_me = row // 4, lax.rem(row, 4)
    sibling = (row + 1 - 2 * core, z)
    hops = ((row, lax.rem(z + 1, NZ)), (row, lax.rem(z + NZ - 1, NZ)))
    k_me = lax.rem(r_me // 2 + d_me // 2, 2) + 2 * lax.rem(r_me + d_me, 2)
    dm = tok.shape[-1]
    ff = gath.shape[-1]
    half = ff // 2

    load_w = pltpu.make_async_copy(w_in, w, load_sem.at[0])
    load_go = pltpu.make_async_copy(go_in, go, load_sem.at[1])
    load_w.start()
    load_go.start()

    def plane(j):
        px = lax.rem(x + j // 4, 4)
        py = lax.rem(y + lax.rem(j, 4), 4)
        return ((px * 4 + py) * 2 + core, z)

    barrier = pltpu.get_barrier_semaphore()
    for there in (*hops, sibling):
        pl.semaphore_signal(barrier, inc=1, device_id=there, device_id_type=MESH)

    def greet(j, _):
        pl.semaphore_signal(barrier, inc=1, device_id=plane(j), device_id_type=MESH)
        return 0

    lax.fori_loop(1, 16, greet, 0)
    pl.semaphore_wait(barrier, 18)

    def slot(d):
        d = lax.rem(d, NZ)
        return lax.rem(d, 2) * 4 + d // 2

    def owner(c, d):
        k = lax.rem(c, 4)
        return 2 * lax.rem(k + d // 2, 2) + lax.rem(k // 2 + d, 2)

    def parity(c, of):
        return lax.rem(of + lax.rem(c, 4) // 2, 2)

    def four(c, of):
        return pl.ds(parity(c, of) * 4, 4)

    def remote(src, dst, send, recv, there):
        return pltpu.make_async_remote_copy(
            src_ref=src, dst_ref=dst, send_sem=send, recv_sem=recv,
            device_id=there, device_id_type=MESH,
        )

    def send_tokens(c):
        h = c // 4

        @pl.when(k_me == lax.rem(c, 4))
        def _():
            mine = tok_in.at[pl.ds(pl.multiple_of(h * TB, TB), TB)]

            def one(j, _):
                remote(mine, tok.at[c, slot(d_me)], tok_send.at[h], tok_recv.at[c], plane(j)).start()
                return 0

            lax.fori_loop(1, 16, one, 0)
            pltpu.make_async_copy(mine, tok.at[c, slot(d_me)], tok_recv.at[c]).start()

    def forward_tokens(c):
        part_of = tok.at[c, four(c, core)]
        return remote(part_of, part_of, fwd_send.at[c], fwd_recv.at[c], sibling)

    def ring_copy(d, c, s):
        if s == 0:
            cols = pl.ds(d * half, half)
            src = part.at[c, slot(z + 4), :, cols]
            dst = ring.at[d, c, 0, :, cols]
        else:
            src, dst = ring.at[d, c, s - 1], ring.at[d, c, s]
        return remote(src, dst, ring_send.at[d, c, s], ring_recv.at[d, c, s], hops[d])

    def gath_copy(d, c, s):
        at = slot(z + (NZ - s if d == 0 else s))
        if s == 3:
            ref = gath.at[c, at, :, pl.ds(d * half, half)]
        else:
            ref = gath.at[c, at]
        return remote(ref, ref, gath_send.at[d, c, s], gath_recv.at[d, c, s], hops[d])

    def fetch(c):
        direct = tok.at[c, four(c, core)]
        pltpu.make_async_copy(direct, direct, tok_recv.at[c]).wait()
        forward_tokens(c).start()

        @pl.when(c + AHEAD < NC)
        def _():
            send_tokens(c + AHEAD)

    def first(c):
        other = tok.at[c, four(c, 1 - core)]
        pltpu.make_async_copy(other, other, fwd_recv.at[c]).wait()
        left = tok[c].reshape(NZ * TB, dm)
        for n in range(ff // 256):
            at = pl.ds(n * 256, 256)
            got = jnp.dot(left, w[:, at], preferred_element_type=F32)
            part[c, :, :, at] = got.astype(BF16).reshape(NZ, TB, 256)
        for d in range(2):
            ring_copy(d, c, 0).start()

    def ring_step(c, s):
        for d in range(2):
            ring_copy(d, c, s - 1).wait_recv()
            at = slot(z + (4 - s if d == 0 else 4 + s))
            if s == 1:
                got, rest = slice(d * half, (d + 1) * half), slice((1 - d) * half, (2 - d) * half)
                total = ring[d, c, 0, :, got].astype(F32) + part[c, at, :, got].astype(F32)
                ring[d, c, 0, :, got] = total.astype(BF16)
                ring[d, c, 0, :, rest] = part[c, at, :, rest]
            else:
                total = ring[d, c, s - 1].astype(F32) + part[c, at].astype(F32)
                ring[d, c, s - 1] = total.astype(BF16)
            ring_copy(d, c, s).start()

    def middle(c):
        @pl.when(c == 0)
        def _():
            load_go.wait()

        for d in range(2):
            ring_copy(d, c, 3).wait_recv()
        at = pl.ds(pl.multiple_of(owner(c, z) * 32 + (c // 4) * TB, TB), TB)
        pre = (
            part[c, slot(z)].astype(F32) + ring[0, c, 3].astype(F32) + ring[1, c, 3].astype(F32)
        )
        hidden, slope = activations(pre)
        hid_out[at, :] = hidden.astype(BF16)
        gath[c, slot(z)] = (go[at, :].astype(F32) * slope).astype(BF16)
        for d in range(2):
            gath_copy(d, c, 0).start()

    def gath_step(c, s):
        for d in range(2):
            gath_copy(d, c, s - 1).wait_recv()
            gath_copy(d, c, s).start()

    def quo_copy(c):
        theirs = quo.at[c, four(c, 1 - core)]
        return remote(theirs, quo_in.at[c], quo_send.at[c], quo_recv.at[c], sibling)

    def back(c):
        for d in range(2):
            gath_copy(d, c, 3).wait_recv()
        left = gath[c].reshape(NZ * TB, ff)

        for n in range(dm // 256):
            at = pl.ds(n * 256, 256)
            got = jnp.dot(left, wt[:, at], preferred_element_type=F32)
            quo[c, :, :, at] = got.astype(BF16).reshape(NZ, TB, 256)
        quo_copy(c).start()

    def scatter(c):
        h, p = c // 4, parity(c, core)
        quo_copy(c).wait_recv()

        def one(j, _):
            at = lax.rem(d_me // 2 + j, 4)
            d = 2 * at + p
            mine = quo.at[c, p * 4 + at]
            total = quo[c, p * 4 + at].astype(F32) + quo_in[c, at].astype(F32)
            quo[c, p * 4 + at] = total.astype(BF16)
            there = d * 4 + owner(c, d)

            @pl.when(there != row)
            def _():
                remote(
                    mine, rs_in.at[h, chip], rs_send.at[c], rs_recv.at[h], (there, z)
                ).start()

            @pl.when(there == row)
            def _():
                pltpu.make_async_copy(mine, rs_in.at[h, chip], rs_recv.at[h]).start()

            return 0

        lax.fori_loop(0, 4, one, 0)

    def weigh(c, n, opening, closing, tiles):
        def tile(m, _):
            at = pl.ds(pl.multiple_of(m * 256, 256), 256)
            left = tok[pl.ds(c, n), :, :, at].reshape(n * NZ * TB, 256)
            for f in range(ff // 512):
                cols = pl.ds(f * 512, 512)
                right = gath[pl.ds(c, n), :, :, cols].reshape(n * NZ * TB, 512)
                got = lax.dot_general(
                    left, right, (((0,), (0,)), ((), ())), preferred_element_type=F32
                )
                if not opening:
                    got = got + acc[at, cols]
                if closing:
                    gw_out[at, cols] = got.astype(BF16)
                else:
                    acc[at, cols] = got
            return 0

        lax.fori_loop(tiles[0], tiles[1], tile, 0)

    def collect(h):
        pltpu.make_async_copy(rs_in.at[h], rs_in.at[h], rs_recv.at[h]).wait()
        total = rs_in[h, 0].astype(F32)
        for j in range(1, 16):
            total = total + rs_in[h, j].astype(F32)
        gt_out[pl.ds(h * TB, TB), :] = total.astype(BF16)

    def turn(n, _):
        at = pl.ds(pl.multiple_of(n * 256, 256), 256)
        wt[:, at] = w[at, :].T
        return 0

    for c in range(AHEAD):
        send_tokens(c)
    load_w.wait()
    lax.fori_loop(0, 4, turn, 0)
    fetch(0)
    lax.fori_loop(4, 6, turn, 0)

    def stage(i, offset, fn):
        c = i - offset

        @pl.when((c >= 0) & (c < NC))
        def _():
            fn(jnp.clip(c, 0, NC - 1))

    def step(i, _):
        stage(i, 1, lambda c: ring_step(c, 1))
        stage(i, 0, first)
        for s in (2, 3):
            stage(i, s, lambda c: ring_step(c, s))
        stage(i, 4, middle)
        for s in (1, 2, 3):
            stage(i, 4 + s, lambda c: gath_step(c, s))
        stage(i, 9, scatter)
        stage(i, 8, back)

        @pl.when(i == 9)
        def _():
            weigh(0, 2, True, False, (0, 6))

        @pl.when(i == 11)
        def _():
            weigh(2, 2, False, False, (0, 6))

        @pl.when(i + 1 < NC)
        def _():
            fetch(i + 1)

        return 0

    lax.fori_loop(0, NC + 8, step, 0)
    weigh(4, 4, False, True, (0, 2))
    scatter(NC - 1)
    weigh(4, 4, False, True, (2, 6))
    collect(0)
    collect(1)

    for h in range(2):
        sent = rs_in.at[h, pl.ds(0, 15)]
        pltpu.make_async_copy(sent, sent, tok_send.at[h]).wait()

    def drain(c, _):
        for d in range(2):
            for s in range(4):
                ring_copy(d, c, s).wait_send()
                gath_copy(d, c, s).wait_send()
        forward_tokens(c).wait_send()
        quo_copy(c).wait_send()

        @pl.when(k_me == lax.rem(c, 4))
        def _():
            sent = quo_in.at[c, pl.ds(0, 3)]
            pltpu.make_async_copy(sent, sent, rs_send.at[c]).wait()

        @pl.when(k_me != lax.rem(c, 4))
        def _():
            sent = quo_in.at[c]
            pltpu.make_async_copy(sent, sent, rs_send.at[c]).wait()

        return 0

    lax.fori_loop(0, NC, drain, 0)


def store(hid, gt, gw, hid_out, gt_out, gw_out, sem):
    copies = [
        pltpu.make_async_copy(src, dst, sem.at[n])
        for n, (src, dst) in enumerate(((gw, gw_out), (hid, hid_out), (gt, gt_out)))
    ]
    for copy in copies:
        copy.start()
    for copy in copies:
        copy.wait()


def local(tokens, weight, grad_out):
    dm, ff = weight.shape
    dma = pltpu.SemaphoreType.DMA
    vmem = pltpu.VMEM
    shapes = (grad_out.shape, tokens.shape, weight.shape)
    held = pl.pallas_call(
        kernel,
        out_shape=tuple(pltpu.VMEM(shape, BF16) for shape in shapes),
        in_specs=[pl.BlockSpec(memory_space=pl.ANY)] * 3,
        out_specs=[pl.BlockSpec(memory_space=pltpu.VMEM)] * 3,
        scratch_shapes=[
            vmem((dm, ff), BF16),
            vmem((ff, dm), BF16),
            vmem(grad_out.shape, BF16),
            vmem((NC, NZ, TB, dm), BF16),
            vmem((NC, NZ, TB, ff), BF16),
            vmem((2, NC, 4, TB, ff), BF16),
            vmem((NC, NZ, TB, ff), BF16),
            vmem((NC, NZ, TB, dm), BF16),
            vmem((NC, 4, TB, dm), BF16),
            vmem((2, 16, TB, dm), BF16),
            vmem((dm, ff), F32),
            dma((2,)), dma((NC,)), dma((NC,)), dma((NC,)),
            dma((2, NC, 4)), dma((2, NC, 4)), dma((2, NC, 4)), dma((2, NC, 4)),
            dma((NC,)), dma((NC,)), dma((NC,)), dma((2,)), dma((2,)),
        ],
        compiler_params=pltpu.CompilerParams(
            collective_id=0, has_side_effects=True, vmem_limit_bytes=56 * 1024 * 1024
        ),
        cost_estimate=pl.CostEstimate(
            flops=6 * 1024 * dm * ff, bytes_accessed=4 * dm * ff, transcendentals=0
        ),
        name="mlp",
    )(tokens, weight, grad_out)
    return pl.pallas_call(
        store,
        out_shape=tuple(jax.ShapeDtypeStruct(shape, BF16) for shape in shapes),
        in_specs=[pl.BlockSpec(memory_space=pltpu.VMEM)] * 3,
        out_specs=[pl.BlockSpec(memory_space=pl.ANY)] * 3,
        scratch_shapes=[dma((3,))],
        compiler_params=pltpu.CompilerParams(vmem_limit_bytes=1024 * 1024),
        name="store",
    )(*(pltpu.with_memory_space_constraint(x, pltpu.VMEM) for x in held))


def solution(mesh):
    placed = (P("row", "col"), P("col", "row"), P("col", "row"))
    return jax.shard_map(
        local,
        mesh=mesh,
        in_specs=placed,
        out_specs=(P("col", "row"), P("row", "col"), P("col", "row")),
        check_vma=False,
    )
```

```python
import math

import jax
import jax.numpy as jnp
from jax import lax
from jax.experimental import pallas as pl
from jax.experimental.pallas import tpu as pltpu
from jax.sharding import PartitionSpec as P

MESH = pl.DeviceIdType.MESH
F32 = jnp.float32
BF16 = jnp.bfloat16
NZ = 8
NC = 8
TB = 16
AHEAD = 3

FAR_FIRST = (10, 9, 11, 8, 6, 14, 2, 5, 13, 7, 15, 4, 12, 1, 3)
PLAN = (
    (11, 3), (11, 4), (11, 5), (10, 0), (0, 0), (10, 1), (0, 1), (10, 2),
    (1, 0), (0, 2), (10, 3), (1, 1), (2, 0), (0, 3), (10, 4), (1, 2),
    (2, 1), (3, 0), (0, 4), (10, 5), (1, 3), (2, 2), (3, 1), (0, 5),
    (10, 6), (4, 0), (1, 4), (2, 3), (3, 2), (10, 7), (0, 6), (4, 1),
    (1, 5), (5, 0), (0, 7), (2, 4), (3, 3), (4, 2), (1, 6), (5, 1),
    (2, 5), (6, 0), (1, 7), (3, 4), (4, 3), (5, 2), (2, 6), (6, 1),
    (3, 5), (7, 0), (2, 7), (4, 4), (5, 3), (6, 2), (3, 6), (7, 1),
    (4, 5), (8, 0), (3, 7), (5, 4), (6, 3), (9, 0), (7, 2), (4, 6),
    (8, 1), (5, 5), (12, 0), (4, 7), (6, 4), (12, 1), (9, 1), (7, 3),
    (8, 2), (5, 6), (12, 2), (6, 5), (12, 3), (5, 7), (12, 4), (9, 2),
    (7, 4), (8, 3), (6, 6), (12, 5), (7, 5), (12, 6), (6, 7), (8, 4),
    (9, 3), (7, 6), (8, 5), (9, 4), (7, 7), (12, 7), (12, 8), (8, 6),
    (9, 5), (12, 9), (8, 7), (9, 6), (12, 10), (12, 11), (12, 12), (12, 13),
    (9, 7), (12, 14), (12, 15), (12, 16), (12, 17), (12, 18), (12, 19), (12, 20),
    (12, 21), (12, 22), (12, 23),
)


def activations(pre):
    coef = math.sqrt(2.0 / math.pi)
    inner = coef * (pre + 0.044715 * pre * pre * pre)
    tval = jnp.tanh(inner)
    hidden = 0.5 * pre * (1.0 + tval)
    slope = 0.5 * (1.0 + tval) + 0.5 * pre * (1.0 - tval * tval) * coef * (
        1.0 + 3.0 * 0.044715 * pre * pre
    )
    return (hidden, slope)


def kernel(
    tok_in, w_in, go_in,
    hid_out, gt_out, gw_out,
    w, wt, go, tok, part, ring, gath, quo, quo_in, rs_in, acc,
    tok_send, tok_recv, fwd_send, fwd_recv, ring_send, ring_recv, gath_send, gath_recv,
    quo_send, quo_recv, rs_send, rs_recv, load_sem,
):
    row = lax.axis_index("row")
    z = lax.axis_index("col")
    core = lax.rem(row, 2)
    chip = row // 2
    x, y = chip // 4, lax.rem(chip, 4)
    d_me, r_me = row // 4, lax.rem(row, 4)
    sibling = (row + 1 - 2 * core, z)
    hops = ((row, lax.rem(z + 1, NZ)), (row, lax.rem(z + NZ - 1, NZ)))
    k_me = lax.rem(r_me // 2 + d_me // 2, 2) + 2 * lax.rem(r_me + d_me, 2)
    dm = tok.shape[-1]
    ff = gath.shape[-1]
    half = ff // 2

    load_w = pltpu.make_async_copy(w_in, w, load_sem.at[0])
    load_go = pltpu.make_async_copy(go_in, go, load_sem.at[1])
    load_w.start()
    load_go.start()

    def plane(j):
        px = lax.rem(x + j // 4, 4)
        py = lax.rem(y + j % 4, 4)
        return ((px * 4 + py) * 2 + core, z)

    barrier = pltpu.get_barrier_semaphore()
    for there in (*hops, sibling):
        pl.semaphore_signal(barrier, inc=1, device_id=there, device_id_type=MESH)

    for j in range(1, 16):
        pl.semaphore_signal(barrier, inc=1, device_id=plane(j), device_id_type=MESH)
    pl.semaphore_wait(barrier, 18)

    def slot(d):
        d = lax.rem(d, NZ)
        return lax.rem(d, 2) * 4 + d // 2

    def owner(c, d):
        k = c % 4
        return 2 * lax.rem(k + d // 2, 2) + lax.rem(k // 2 + d, 2)

    def parity(c, of):
        return lax.rem(of + c % 4 // 2, 2)

    def four(c, of):
        return pl.ds(parity(c, of) * 4, 4)

    def remote(src, dst, send, recv, there):
        return pltpu.make_async_remote_copy(
            src_ref=src, dst_ref=dst, send_sem=send, recv_sem=recv,
            device_id=there, device_id_type=MESH,
        )

    def send_tokens(c):
        h = c // 4

        @pl.when(k_me == c % 4)
        def _():
            mine = tok_in.at[pl.ds(pl.multiple_of(h * TB, TB), TB)]

            for j in FAR_FIRST:
                remote(mine, tok.at[c, slot(d_me)], tok_send.at[h], tok_recv.at[c], plane(j)).start()
            pltpu.make_async_copy(mine, tok.at[c, slot(d_me)], tok_recv.at[c]).start()

    def forward_tokens(c):
        part_of = tok.at[c, four(c, core)]
        return remote(part_of, part_of, fwd_send.at[c], fwd_recv.at[c], sibling)

    def ring_copy(d, c, s):
        if s == 0:
            cols = pl.ds(d * half, half)
            src = part.at[c, slot(z + 4), :, cols]
            dst = ring.at[d, c, 0, :, cols]
        else:
            src, dst = ring.at[d, c, s - 1], ring.at[d, c, s]
        return remote(src, dst, ring_send.at[d, c, s], ring_recv.at[d, c, s], hops[d])

    def gath_copy(d, c, s):
        at = slot(z + (NZ - s if d == 0 else s))
        if s == 3:
            ref = gath.at[c, at, :, pl.ds(d * half, half)]
        else:
            ref = gath.at[c, at]
        return remote(ref, ref, gath_send.at[d, c, s], gath_recv.at[d, c, s], hops[d])

    def fetch(c):
        direct = tok.at[c, four(c, core)]
        pltpu.make_async_copy(direct, direct, tok_recv.at[c]).wait()
        forward_tokens(c).start()

        if c + AHEAD < NC:
            send_tokens(c + AHEAD)

    def first(c):
        other = tok.at[c, four(c, 1 - core)]
        pltpu.make_async_copy(other, other, fwd_recv.at[c]).wait()
        left = tok[c].reshape(NZ * TB, dm)
        for n in range(ff // 256):
            at = pl.ds(n * 256, 256)
            got = jnp.dot(left, w[:, at], preferred_element_type=F32)
            part[c, :, :, at] = got.astype(BF16).reshape(NZ, TB, 256)
        for d in range(2):
            ring_copy(d, c, 0).start()

    def ring_step(c, s):
        for d in range(2):
            ring_copy(d, c, s - 1).wait_recv()
            at = slot(z + (4 - s if d == 0 else 4 + s))
            if s == 1:
                got, rest = slice(d * half, (d + 1) * half), slice((1 - d) * half, (2 - d) * half)
                total = ring[d, c, 0, :, got].astype(F32) + part[c, at, :, got].astype(F32)
                ring[d, c, 0, :, got] = total.astype(BF16)
                ring[d, c, 0, :, rest] = part[c, at, :, rest]
            else:
                total = ring[d, c, s - 1].astype(F32) + part[c, at].astype(F32)
                ring[d, c, s - 1] = total.astype(BF16)
            ring_copy(d, c, s).start()

    def middle(c):
        if c == 0:
            load_go.wait()

        for d in range(2):
            ring_copy(d, c, 3).wait_recv()
        at = pl.ds(pl.multiple_of(owner(c, z) * 32 + (c // 4) * TB, TB), TB)
        pre = (
            part[c, slot(z)].astype(F32) + ring[0, c, 3].astype(F32) + ring[1, c, 3].astype(F32)
        )
        hidden, slope = activations(pre)
        hid_out[at, :] = hidden.astype(BF16)
        gath[c, slot(z)] = (go[at, :].astype(F32) * slope).astype(BF16)
        for d in range(2):
            gath_copy(d, c, 0).start()

    def gath_step(c, s):
        for d in range(2):
            gath_copy(d, c, s - 1).wait_recv()
            gath_copy(d, c, s).start()

    def quo_copy(c):
        theirs = quo.at[c, four(c, 1 - core)]
        return remote(theirs, quo_in.at[c], quo_send.at[c], quo_recv.at[c], sibling)

    def back(c):
        for d in range(2):
            gath_copy(d, c, 3).wait_recv()
        left = gath[c].reshape(NZ * TB, ff)

        for n in range(dm // 256):
            at = pl.ds(n * 256, 256)
            got = jnp.dot(left, wt[:, at], preferred_element_type=F32)
            quo[c, :, :, at] = got.astype(BF16).reshape(NZ, TB, 256)
        quo_copy(c).start()

    def scatter(c):
        h, p = c // 4, parity(c, core)
        quo_copy(c).wait_recv()

        def one(j):
            at = lax.rem(x + j, 4)
            d = 2 * at + p
            mine = quo.at[c, p * 4 + at]
            total = quo[c, p * 4 + at].astype(F32) + quo_in[c, at].astype(F32)
            quo[c, p * 4 + at] = total.astype(BF16)
            there = d * 4 + owner(c, d)

            @pl.when(there != row)
            def _():
                remote(
                    mine, rs_in.at[h, chip], rs_send.at[c], rs_recv.at[h], (there, z)
                ).start()

            @pl.when(there == row)
            def _():
                pltpu.make_async_copy(mine, rs_in.at[h, chip], rs_recv.at[h]).start()

        for j in (2, 1, 3, 0):
            one(j)

    def weigh(pair, m):
        at = pl.ds(m * 256, 256)
        left = tok[pl.ds(2 * pair, 2), :, :, at].reshape(2 * NZ * TB, 256)
        for f in range(ff // 512):
            cols = pl.ds(f * 512, 512)
            right = gath[pl.ds(2 * pair, 2), :, :, cols].reshape(2 * NZ * TB, 512)
            got = lax.dot_general(
                left, right, (((0,), (0,)), ((), ())), preferred_element_type=F32
            )
            if pair > 0:
                got = got + acc[at, cols]
            if 2 * pair + 2 == NC:
                gw_out[at, cols] = got.astype(BF16)
            else:
                acc[at, cols] = got

    def collect(h):
        pltpu.make_async_copy(rs_in.at[h], rs_in.at[h], rs_recv.at[h]).wait()
        total = rs_in[h, 0].astype(F32)
        for j in range(1, 16):
            total = total + rs_in[h, j].astype(F32)
        gt_out[pl.ds(h * TB, TB), :] = total.astype(BF16)

    def turn(n):
        at = pl.ds(n * 256, 256)
        wt[:, at] = w[at, :].T

    send_tokens(0)
    load_w.wait()
    turn(0)
    send_tokens(1)
    turn(1)
    turn(2)
    send_tokens(2)
    for kind, c in PLAN:
        if kind == 0:
            first(c)
        elif kind < 4:
            ring_step(c, kind)
        elif kind == 4:
            middle(c)
        elif kind < 8:
            gath_step(c, kind - 4)
        elif kind == 8:
            back(c)
        elif kind == 9:
            scatter(c)
        elif kind == 10:
            fetch(c)
        elif kind == 11:
            turn(c)
        else:
            weigh(c // 6, c % 6)
    collect(0)
    collect(1)

    for h in range(2):
        sent = rs_in.at[h, pl.ds(0, 15)]
        pltpu.make_async_copy(sent, sent, tok_send.at[h]).wait()

    def drain(c):
        for d in range(2):
            for s in range(4):
                ring_copy(d, c, s).wait_send()
                gath_copy(d, c, s).wait_send()
        forward_tokens(c).wait_send()
        quo_copy(c).wait_send()

        @pl.when(k_me == c % 4)
        def _():
            sent = quo_in.at[c, pl.ds(0, 3)]
            pltpu.make_async_copy(sent, sent, rs_send.at[c]).wait()

        @pl.when(k_me != c % 4)
        def _():
            sent = quo_in.at[c]
            pltpu.make_async_copy(sent, sent, rs_send.at[c]).wait()

    for c in range(NC):
        drain(c)


def store(hid, gt, gw, hid_out, gt_out, gw_out, sem):
    copies = [
        pltpu.make_async_copy(src, dst, sem.at[n])
        for n, (src, dst) in enumerate(((gw, gw_out), (hid, hid_out), (gt, gt_out)))
    ]
    for copy in copies:
        copy.start()
    for copy in copies:
        copy.wait()


def local(tokens, weight, grad_out):
    dm, ff = weight.shape
    dma = pltpu.SemaphoreType.DMA
    vmem = pltpu.VMEM
    shapes = (grad_out.shape, tokens.shape, weight.shape)
    held = pl.pallas_call(
        kernel,
        out_shape=tuple(pltpu.VMEM(shape, BF16) for shape in shapes),
        in_specs=[pl.BlockSpec(memory_space=pl.ANY)] * 3,
        out_specs=[pl.BlockSpec(memory_space=pltpu.VMEM)] * 3,
        scratch_shapes=[
            vmem((dm, ff), BF16),
            vmem((ff, dm), BF16),
            vmem(grad_out.shape, BF16),
            vmem((NC, NZ, TB, dm), BF16),
            vmem((NC, NZ, TB, ff), BF16),
            vmem((2, NC, 4, TB, ff), BF16),
            vmem((NC, NZ, TB, ff), BF16),
            vmem((NC, NZ, TB, dm), BF16),
            vmem((NC, 4, TB, dm), BF16),
            vmem((2, 16, TB, dm), BF16),
            vmem((dm, ff), F32),
            dma((2,)), dma((NC,)), dma((NC,)), dma((NC,)),
            dma((2, NC, 4)), dma((2, NC, 4)), dma((2, NC, 4)), dma((2, NC, 4)),
            dma((NC,)), dma((NC,)), dma((NC,)), dma((2,)), dma((2,)),
        ],
        compiler_params=pltpu.CompilerParams(
            collective_id=0, has_side_effects=True, vmem_limit_bytes=56 * 1024 * 1024
        ),
        cost_estimate=pl.CostEstimate(
            flops=6 * 1024 * dm * ff, bytes_accessed=4 * dm * ff, transcendentals=0
        ),
        name="mlp",
    )(tokens, weight, grad_out)
    return pl.pallas_call(
        store,
        out_shape=tuple(jax.ShapeDtypeStruct(shape, BF16) for shape in shapes),
        in_specs=[pl.BlockSpec(memory_space=pltpu.VMEM)] * 3,
        out_specs=[pl.BlockSpec(memory_space=pl.ANY)] * 3,
        scratch_shapes=[dma((3,))],
        compiler_params=pltpu.CompilerParams(vmem_limit_bytes=1024 * 1024),
        name="store",
    )(*(pltpu.with_memory_space_constraint(x, pltpu.VMEM) for x in held))


def solution(mesh):
    placed = (P("row", "col"), P("col", "row"), P("col", "row"))
    return jax.shard_map(
        local,
        mesh=mesh,
        in_specs=placed,
        out_specs=(P("col", "row"), P("row", "col"), P("col", "row")),
        check_vma=False,
    )
```
